32 devices in a mesh: scenes: 2 (over y), rows: 4 (over x, core), cols: 4 (over z).
Axes of the slice: x: 2, y: 2, z: 4, core: 2. Of those that a mesh axis runs over, the one named last changes fastest.
Arguments:
- features: bfloat16 [256, 64, 256], P(('scenes', 'rows'), 'cols'), parts along dimension 0, may hold values from -100 to 100
- dw_kernel: bfloat16 [7, 7, 256], replicated, may hold values from -0.875 to 0.875
- norm_gain: float32 [256], replicated, may hold values from 0.1 to 1.9
- query_state: bfloat16 [600, 256], P('scenes'), parts along dimension 0, may hold values from -6 to 6
- query_pos: bfloat16 [600, 256], P('scenes'), parts along dimension 0, may hold values from -175 to 175
- w_query: bfloat16 [256, 256], replicated, may hold values from -0.375 to 0.375
- w_key: bfloat16 [256, 256], replicated, may hold values from -0.375 to 0.375
- w_value: bfloat16 [256, 256], replicated, may hold values from -0.375 to 0.375
- w_out: bfloat16 [256, 256], replicated, may hold values from -0.375 to 0.375
Outputs:
- memory: bfloat16 [256, 64, 256], P(('scenes', 'rows'), 'cols'), parts along dimension 0
- decoded: float32 [600, 256], P('scenes'), parts along dimension 0
The draws below stay inside these ranges and needn't reach their ends.
There are 2 independent parts, one for each index of `scenes`. The reference program is written for one: setup_inputs(seed, part) draws one part's arguments, and reference() takes and returns one part's arrays. A program takes and returns all parts, laid end to end along the dimension named above; an argument that names none is the same for every part. Nothing has to cross between parts.
All inputs are finite; a program needn't handle non-finite values.
Results may differ from the reference program's by a relative error of at most 0.0024.
The reference program's roundings to bfloat16 on the way (of `mixed`, `queries`, `rounded` and `attended`) count: a program that leaves them out, or rounds other values in their place, can miss the bound.
Values may be sent and summed in bfloat16 or wider, within the bound.
A program may use at most 64 MiB of HBM per device.

```python
import math
import jax
import jax.numpy as jnp
from jax import lax

C = 256
HEADS = 8
NQ = 300
H = 128
W = 64


def draw_features(key, part):
    key_base, key_chan, key_pixel = jax.random.split(key, 3)
    base = jnp.clip(jax.random.normal(key_base, (H, W, C), jnp.float32), -6.0, 6.0)
    chan_scale = jnp.exp(jax.random.uniform(key_chan, (C,), jnp.float32, math.log(0.4), math.log(4.0)))
    pixel_scale = jnp.exp(jax.random.uniform(key_pixel, (H, W, 1), jnp.float32, math.log(0.4), math.log(4.0)))
    return (base * chan_scale * pixel_scale).astype(jnp.bfloat16)


def draw_query_pos(key, part):
    key_base = jax.random.fold_in(key, 0)
    return (2.5 * jnp.clip(jax.random.normal(key_base, (NQ, C), jnp.float32), -6.0, 6.0)).astype(jnp.bfloat16)


def noise(stream_key, shape, deviation, most, held_as=jnp.bfloat16):
    values = jax.random.normal(stream_key, shape, jnp.float32) * deviation
    return jnp.minimum(jnp.maximum(values, -most), most).astype(held_as)


def setup_inputs(seed: int = 0, part: int = 0) -> dict:
    arg_keys = jax.random.split(jax.random.key(seed), 10)
    part_splits = jax.random.split(jax.random.fold_in(arg_keys[9], part), 10)
    features = draw_features(jax.random.fold_in(jax.random.fold_in(arg_keys[9], part), 71), part)
    dw_kernel = noise(arg_keys[1], (7, 7, C), 49 ** -0.5, 0.875)
    norm_gain = jnp.clip(1.0 + 0.18 * jax.random.normal(arg_keys[2], (C,), jnp.float32), 0.1, 1.9)
    query_state = noise(part_splits[3], (NQ, C), 1.0, 6.0)
    query_pos = draw_query_pos(jax.random.fold_in(jax.random.fold_in(arg_keys[9], part), 71), part)
    w_query = noise(arg_keys[5], (C, C), C ** -0.5, 0.375)
    w_key = noise(arg_keys[6], (C, C), C ** -0.5, 0.375)
    w_value = noise(arg_keys[7], (C, C), C ** -0.5, 0.375)
    w_out = noise(arg_keys[8], (C, C), C ** -0.5, 0.375)
    return dict(features=features, dw_kernel=dw_kernel, norm_gain=norm_gain, query_state=query_state, query_pos=query_pos, w_query=w_query, w_key=w_key, w_value=w_value, w_out=w_out)


def layer_norm(vector):
    centred = vector - lax.optimization_barrier(jnp.mean(vector, axis=-1, keepdims=True))
    variance = lax.optimization_barrier(jnp.mean(centred * centred, axis=-1, keepdims=True))
    return centred * lax.rsqrt(variance + 1e-06)

def reference(features, dw_kernel, norm_gain, query_state, query_pos, w_query, w_key, w_value, w_out):
    width = features.shape[-1]
    head_dim = width // HEADS
    image = features.astype(jnp.float32)
    kernel = dw_kernel.astype(jnp.float32)[:, :, None, :]
    conv = lax.conv_general_dilated(image[None], kernel, (1, 1), ((3, 3), (3, 3)), dimension_numbers=('NHWC', 'HWIO', 'NHWC'), feature_group_count=width, precision=lax.Precision.HIGHEST)[0]
    memory = (image + layer_norm(conv) * norm_gain.astype(jnp.float32)).astype(jnp.bfloat16)
    flat = memory.reshape(-1, width)
    keys = jnp.dot(flat, w_key, preferred_element_type=jnp.float32).astype(jnp.bfloat16)
    values = jnp.dot(flat, w_value, preferred_element_type=jnp.float32).astype(jnp.bfloat16)
    mixed = (query_state.astype(jnp.float32) + query_pos.astype(jnp.float32)).astype(jnp.bfloat16)
    queries = (jnp.dot(mixed, w_query, preferred_element_type=jnp.float32) * head_dim ** (-0.5)).astype(jnp.bfloat16)
    q_heads = queries.astype(jnp.float32).reshape(NQ, HEADS, head_dim)
    pixels = flat.shape[0]
    block_size = math.gcd(pixels, 16384)
    count = pixels // block_size
    key_blocks = keys.reshape(count, block_size, HEADS, head_dim)
    value_blocks = values.reshape(count, block_size, HEADS, head_dim)

    def block_scores(key_block):
        return jnp.einsum('qhd,phd->hqp', q_heads, key_block.astype(jnp.float32), precision=lax.Precision.HIGHEST)

    def block_max(key_block):
        return lax.optimization_barrier(jnp.max(block_scores(key_block), axis=-1))
    maxima = lax.optimization_barrier(jnp.max(lax.map(block_max, key_blocks), axis=0))

    def accumulate(carry, pair):
        totals, sums = carry
        key_block, value_block = pair
        expo = jnp.exp(block_scores(key_block) - maxima[:, :, None])
        rounded = lax.optimization_barrier(expo.astype(jnp.bfloat16)).astype(jnp.float32)
        sums = sums + jnp.einsum('hqp,phd->qhd', rounded, value_block.astype(jnp.float32), precision=lax.Precision.HIGHEST)
        return ((totals + lax.optimization_barrier(jnp.sum(expo, axis=-1)), sums), None)
    start = (jnp.zeros((HEADS, NQ), jnp.float32), jnp.zeros((NQ, HEADS, head_dim), jnp.float32))
    (totals, sums), unused = lax.scan(accumulate, start, (key_blocks, value_blocks))
    attended = (sums / totals.T[:, :, None]).reshape(NQ, width).astype(jnp.bfloat16)
    projected = jnp.dot(attended, w_out, preferred_element_type=jnp.float32)
    decoded = layer_norm(query_state.astype(jnp.float32) + projected)
    return (memory, decoded)
```

```python
import functools
import jax
import jax.numpy as jnp
from jax import lax
from jax.experimental import pallas as pl
from jax.experimental.pallas import tpu as pltpu
from jax.sharding import PartitionSpec as P

HEADS = 8
SCATTER = "rows"
EXCHANGE = "cols"
MESH = pl.DeviceIdType.MESH
F32 = jnp.float32
BF16 = jnp.bfloat16
STATS = 128

DIRS = ((-1, 0), (1, 0), (0, -1), (0, 1), (-1, -1), (-1, 1), (1, -1), (1, 1))


def iota(shape, dim):
    return lax.broadcasted_iota(jnp.int32, shape, dim)


def layer_norm(vector):
    centred = vector - jnp.mean(vector, axis=-1, keepdims=True)
    variance = jnp.mean(centred * centred, axis=-1, keepdims=True)
    return centred * lax.rsqrt(variance + 1e-06)


def dot(a, b):
    return jnp.dot(a, b, preferred_element_type=F32)


def split(value, terms):
    parts = []
    for _ in range(terms):
        part = value.astype(BF16)
        parts.append(part)
        value = value - part.astype(F32)
    return parts


def pack(out_ref, sums, maxima, totals):
    width = sums.shape[1]
    head_dim = width // HEADS
    out_ref[:, :width] = sums.astype(BF16)
    src, lane = iota((width, STATS), 0), iota((width, STATS), 1)
    stats = None
    for group, part in enumerate(split(maxima, 3) + split(totals, 3)):
        pick = (src == (lane - group * HEADS) * head_dim) & (lane >= group * HEADS)
        pick = pick & (lane < (group + 1) * HEADS)
        term = dot(part, jnp.where(pick, 1.0, 0.0).astype(BF16))
        stats = term if stats is None else stats + term
    out_ref[:, width:] = stats.astype(BF16)


def unpack(in_ref, width):
    head_dim = width // HEADS
    sums = in_ref[:, :width].astype(F32)
    stats = in_ref[:, width:]
    lane, chan = iota((STATS, width), 0), iota((STATS, width), 1)
    results = [sums]
    for first in (0, 3 * HEADS):
        pick = None
        for group in range(3):
            head = lane - (first + group * HEADS)
            hit = (chan >= head * head_dim) & (chan < (head + 1) * head_dim)
            hit = hit & (head >= 0) & (head < HEADS)
            pick = hit if pick is None else pick | hit
        results.append(dot(stats, jnp.where(pick, 1.0, 0.0).astype(BF16)))
    return results


def combine(parts):
    top = parts[0][1]
    for _, maxima, _ in parts[1:]:
        top = jnp.maximum(top, maxima)
    sums, totals = None, None
    for part_sums, maxima, part_totals in parts:
        scale = jnp.exp(maxima - top)
        s, t = part_sums * scale, part_totals * scale
        sums = s if sums is None else sums + s
        totals = t if totals is None else totals + t
    return sums, top, totals


def kernel(
    sizes, feat, dwk, gain, qs, qp, wq, wk, wv, wo, mem, dec,
    pad, dwf, conv, packed, rowrecv, colrecv, cornrecv, keys, values, qf, queries,
    p1send, p1recv, p2send, p2recv, attended,
    hsend, hrecv, s1, r1, s2, r2, s3, r3,
):
    n_rows, n_cols = sizes["rows"], sizes["cols"]
    n_a, n_b = sizes[SCATTER], sizes[EXCHANGE]
    tile_rows, tile_cols, width = feat.shape
    pixels = tile_rows * tile_cols
    n_query = qs.shape[0]
    block = p2send.shape[0]
    head_dim = width // HEADS
    row, col = lax.axis_index("rows"), lax.axis_index("cols")
    me_a, me_b = lax.axis_index(SCATTER), lax.axis_index(EXCHANGE)

    barrier = pltpu.get_barrier_semaphore()
    for k in range(1, n_a):
        pl.semaphore_signal(
            barrier, inc=1, device_id={SCATTER: lax.rem(me_a + k, n_a)}, device_id_type=MESH
        )
    for k in range(1, n_b):
        pl.semaphore_signal(
            barrier, inc=1, device_id={EXCHANGE: lax.rem(me_b + k, n_b)}, device_id_type=MESH
        )
    for dr, dc in DIRS[4:]:
        pl.semaphore_signal(
            barrier, inc=1,
            device_id={
                "rows": lax.rem(row + dr + n_rows, n_rows),
                "cols": lax.rem(col + dc + n_cols, n_cols),
            },
            device_id_type=MESH,
        )

    flat_in = feat[...].reshape(pixels, width)
    pieces = []
    for first in (0, tile_cols - 3):
        for j in range(3):
            want = iota((tile_rows, pixels), 0) * tile_cols + (first + j)
            pieces.append(want == iota((tile_rows, pixels), 1))
    for dr, dc in DIRS[4:]:
        k = iota((16, pixels), 0)
        i, j = k >> 2, k & 3
        r0 = 0 if dr < 0 else tile_rows - 3
        c0 = 0 if dc < 0 else tile_cols - 3
        want = (r0 + i) * tile_cols + c0 + j
        pieces.append((want == iota((16, pixels), 1)) & (i < 3) & (j < 3))
    select = jnp.concatenate([jnp.where(p, 1.0, 0.0).astype(BF16) for p in pieces], axis=0)
    packed[...] = dot(select, flat_in).astype(BF16)

    pl.semaphore_wait(barrier, (n_a - 1) + (n_b - 1) + 4)

    def halo(index):
        dr, dc = DIRS[index]
        if index < 2:
            src = feat.at[pl.ds(0 if dr < 0 else tile_rows - 3, 3)]
            dst = rowrecv.at[index]
        elif index < 4:
            src = packed.at[pl.ds((index - 2) * 3 * tile_rows, 3 * tile_rows)]
            dst = colrecv.at[index - 2]
        else:
            src = packed.at[pl.ds(6 * tile_rows + (index - 4) * 16, 16)]
            dst = cornrecv.at[index - 4]
        there = (
            (row + dr >= 0) & (row + dr < n_rows) & (col + dc >= 0) & (col + dc < n_cols)
        )
        comes = (
            (row - dr >= 0) & (row - dr < n_rows) & (col - dc >= 0) & (col - dc < n_cols)
        )
        copy = pltpu.make_async_remote_copy(
            src_ref=src, dst_ref=dst, send_sem=hsend.at[index], recv_sem=hrecv.at[index],
            device_id={"rows": row + dr, "cols": col + dc}, device_id_type=MESH,
        )
        return copy, there, comes, dst

    halos = [halo(i) for i in range(8)]
    for index in (2, 3, 4, 5, 6, 7, 0, 1):
        copy, there, comes, dst = halos[index]

        @pl.when(there)
        def _():
            copy.start()

        @pl.when(jnp.logical_not(comes))
        def _():
            dst[...] = jnp.zeros(dst.shape, BF16)

    pad[pl.ds(3, tile_rows), 8 : 8 + tile_cols, :] = feat[...].astype(F32)
    dwf[...] = dwk[...].astype(F32)
    mixed = (qs[...].astype(F32) + qp[...].astype(F32)).astype(BF16)
    qf[...] = jnp.zeros(qf.shape, F32)
    qf[0:n_query, :] = dot(mixed, wq[...]) * head_dim ** (-0.5)
    queries[...] = qf[...].astype(BF16)

    for index in range(8):
        copy, there, comes, dst = halos[index]

        @pl.when(comes)
        def _():
            copy.wait_recv()

    for index in range(2):
        at = 0 if DIRS[index][0] > 0 else tile_rows + 3
        pad[at : at + 3, 8 : 8 + tile_cols, :] = rowrecv[index].astype(F32)
    for index in range(2, 4):
        k, q = iota((tile_rows * 8, 3 * tile_rows), 1), iota((tile_rows * 8, 3 * tile_rows), 0)
        j = jnp.where(k >= tile_rows, 1, 0) + jnp.where(k >= 2 * tile_rows, 1, 0)
        left = DIRS[index][1] > 0
        hit = q == (k - j * tile_rows) * 8 + j + (5 if left else 0)
        slab = dot(jnp.where(hit, 1.0, 0.0).astype(BF16), colrecv[index - 2])
        at = 0 if left else 8 + tile_cols
        pad[3 : 3 + tile_rows, at : at + 8, :] = slab.reshape(tile_rows, 8, width)
    for index in range(4, 8):
        k, q = iota((24, 16), 1), iota((24, 16), 0)
        left = DIRS[index][1] > 0
        hit = (q == (k >> 2) * 8 + (k & 3) + (5 if left else 0)) & (k < 12) & ((k & 3) < 3)
        slab = dot(jnp.where(hit, 1.0, 0.0).astype(BF16), cornrecv[index - 4])
        up = 0 if DIRS[index][0] > 0 else tile_rows + 3
        at = 0 if left else 8 + tile_cols
        pad[up : up + 3, at : at + 8, :] = slab.reshape(3, 8, width)

    chunk = 8
    scale = gain[...]

    def conv_chunk(step, carry):
        r0 = step * chunk
        for g in range(tile_cols // 8):
            acc = [jnp.zeros((8, width), F32) for _ in range(chunk)]
            for dc in range(7):
                taps = [
                    jnp.broadcast_to(dwf[dr, dc : dc + 1, :], (8, width)) for dr in range(7)
                ]
                for i in range(chunk + 6):
                    x = pad[r0 + i, 5 + dc + 8 * g : 13 + dc + 8 * g, :]
                    for dr in range(7):
                        o = i - dr
                        if 0 <= o < chunk:
                            acc[o] = acc[o] + x * taps[dr]
            for o in range(chunk):
                conv[o, 8 * g : 8 * g + 8, :] = acc[o]
        normed = layer_norm(conv[...].reshape(chunk * tile_cols, width))
        image = feat[pl.ds(r0, chunk)].astype(F32).reshape(chunk * tile_cols, width)
        result = (image + normed * scale).astype(BF16)
        mem[pl.ds(r0, chunk)] = result.reshape(chunk, tile_cols, width)
        return carry

    lax.fori_loop(0, tile_rows // chunk, conv_chunk, 0)

    flat = mem[...].reshape(pixels, width)
    keys[...] = dot(flat, wk[...]).astype(BF16)
    values[...] = dot(flat, wv[...]).astype(BF16)

    def attend(index):
        q = queries[pl.ds(pl.multiple_of(index * block, 16), block), :]
        head_of = iota((block, width), 1) // head_dim
        spread = jnp.concatenate(
            [jnp.where(head_of == h, q, jnp.zeros_like(q)) for h in range(HEADS)], axis=0
        )
        scores = lax.dot_general(
            spread, keys[...], (((1,), (1,)), ((), ())), preferred_element_type=F32
        )
        top = jnp.max(scores, axis=-1, keepdims=True)
        expo = jnp.exp(scores - top)
        total = jnp.sum(expo, axis=-1, keepdims=True)
        out = dot(expo.astype(BF16), values[...])
        sums = jnp.zeros((block, width), F32)
        maxima = jnp.zeros((block, width), F32)
        totals = jnp.zeros((block, width), F32)
        for h in range(HEADS):
            rows = slice(h * block, (h + 1) * block)
            here = head_of == h
            sums = jnp.where(here, out[rows], sums)
            maxima = jnp.where(here, top[rows], maxima)
            totals = jnp.where(here, total[rows], totals)
        return sums, maxima, totals

    def p1(k):
        return pltpu.make_async_remote_copy(
            src_ref=p1send.at[k - 1], dst_ref=p1recv.at[k - 1],
            send_sem=s1.at[k - 1], recv_sem=r1.at[k - 1],
            device_id={SCATTER: lax.rem(me_a + k, n_a)}, device_id_type=MESH,
        )

    def scatter_step(step, carry):
        k = step + 1
        pack(p1send.at[step], *attend(lax.rem(me_a + k, n_a)))
        p1(k).start()
        return carry

    lax.fori_loop(0, n_a - 1, scatter_step, 0)
    parts = [attend(me_a)]
    for k in range(1, n_a):
        p1(k).wait_recv()
        parts.append(unpack(p1recv.at[k - 1], width))
    mine = combine(parts)
    pack(p2send, *mine)

    def p2(k):
        return pltpu.make_async_remote_copy(
            src_ref=p2send, dst_ref=p2recv.at[k - 1],
            send_sem=s2.at[k - 1], recv_sem=r2.at[k - 1],
            device_id={EXCHANGE: lax.rem(me_b + k, n_b)}, device_id_type=MESH,
        )

    for k in range(1, n_b):
        p2(k).start()
    parts = [unpack(p2send, width)]
    for k in range(1, n_b):
        p2(k).wait_recv()
        parts.append(unpack(p2recv.at[k - 1], width))
    sums, _, totals = combine(parts)
    attended[me_a] = (sums / totals).astype(BF16)

    def p3(k):
        return pltpu.make_async_remote_copy(
            src_ref=attended.at[me_a], dst_ref=attended.at[me_a],
            send_sem=s3.at[k - 1], recv_sem=r3.at[k - 1],
            device_id={SCATTER: lax.rem(me_a + k, n_a)}, device_id_type=MESH,
        )

    for k in range(1, n_a):
        p3(k).start()
    for k in range(1, n_a):
        p3(k).wait_recv()
    projected = dot(attended[...].reshape(n_a * block, width), wo[...])
    dec[...] = layer_norm(qs[...].astype(F32) + projected[:n_query])

    for index in range(8):
        copy, there, comes, dst = halos[index]

        @pl.when(there)
        def _():
            copy.wait_send()

    for k in range(1, n_a):
        p1(k).wait_send()
        p3(k).wait_send()
    for k in range(1, n_b):
        p2(k).wait_send()


def body(sizes, features, dw_kernel, norm_gain, query_state, query_pos, wq, wk, wv, wo):
    tile_rows, tile_cols, width = features.shape
    n_query = query_state.shape[0]
    n_a, n_b = sizes[SCATTER], sizes[EXCHANGE]
    block = -(-n_query // (16 * n_a)) * 16
    pixels = tile_rows * tile_cols
    row_bytes = width + STATS
    vmem = pl.BlockSpec(memory_space=pltpu.VMEM)
    dma = pltpu.SemaphoreType.DMA
    return pl.pallas_call(
        functools.partial(kernel, sizes),
        out_shape=(
            jax.ShapeDtypeStruct(features.shape, BF16),
            jax.ShapeDtypeStruct((n_query, width), F32),
        ),
        in_specs=[vmem] * 9,
        out_specs=(vmem, vmem),
        scratch_shapes=[
            pltpu.VMEM((tile_rows + 6, tile_cols + 16, width), F32),
            pltpu.VMEM((7, 7, width), F32),
            pltpu.VMEM((8, tile_cols, width), F32),
            pltpu.VMEM((6 * tile_rows + 64, width), BF16),
            pltpu.VMEM((2, 3, tile_cols, width), BF16),
            pltpu.VMEM((2, 3 * tile_rows, width), BF16),
            pltpu.VMEM((4, 16, width), BF16),
            pltpu.VMEM((pixels, width), BF16),
            pltpu.VMEM((pixels, width), BF16),
            pltpu.VMEM((n_a * block, width), F32),
            pltpu.VMEM((n_a * block, width), BF16),
            pltpu.VMEM((n_a - 1, block, row_bytes), BF16),
            pltpu.VMEM((n_a - 1, block, row_bytes), BF16),
            pltpu.VMEM((block, row_bytes), BF16),
            pltpu.VMEM((n_b - 1, block, row_bytes), BF16),
            pltpu.VMEM((n_a, block, width), BF16),
            dma((8,)), dma((8,)),
            dma((n_a - 1,)), dma((n_a - 1,)),
            dma((n_b - 1,)), dma((n_b - 1,)),
            dma((n_a - 1,)), dma((n_a - 1,)),
        ],
        compiler_params=pltpu.CompilerParams(
            collective_id=0, has_side_effects=True, vmem_limit_bytes=40 * 1024 * 1024
        ),
    )(features, dw_kernel, norm_gain.reshape(1, width), query_state, query_pos, wq, wk, wv, wo)


def solution(mesh):
    sizes = dict(mesh.shape)
    in_specs = (
        P(("scenes", "rows"), "cols", None),
        P(),
        P(),
        P("scenes", None),
        P("scenes", None),
        P(),
        P(),
        P(),
        P(),
    )
    out_specs = (P(("scenes", "rows"), "cols", None), P("scenes", None))
    return jax.shard_map(
        functools.partial(body, sizes), mesh=mesh, in_specs=in_specs, out_specs=out_specs,
        check_vma=False,
    )
```

```python
import functools
import jax
import jax.numpy as jnp
from jax import lax
from jax.experimental import pallas as pl
from jax.experimental.pallas import tpu as pltpu
from jax.sharding import PartitionSpec as P

HEADS = 8
SCATTER = "rows"
EXCHANGE = "cols"
MESH = pl.DeviceIdType.MESH
F32 = jnp.float32
BF16 = jnp.bfloat16
STATS = 128

DIRS = ((-1, 0), (1, 0), (0, -1), (0, 1), (-1, -1), (-1, 1), (1, -1), (1, 1))


def iota(shape, dim):
    return lax.broadcasted_iota(jnp.int32, shape, dim)


def layer_norm(vector):
    centred = vector - jnp.mean(vector, axis=-1, keepdims=True)
    variance = jnp.mean(centred * centred, axis=-1, keepdims=True)
    return centred * lax.rsqrt(variance + 1e-06)


def dot(a, b):
    return jnp.dot(a, b, preferred_element_type=F32)


def split(value, terms):
    parts = []
    for _ in range(terms):
        part = value.astype(BF16)
        parts.append(part)
        value = value - part.astype(F32)
    return parts


def pack(out_ref, sums, maxima, totals):
    width = sums.shape[1]
    head_dim = width // HEADS
    out_ref[:, :width] = sums.astype(BF16)
    src, lane = iota((width, STATS), 0), iota((width, STATS), 1)
    stats = None
    for group, part in enumerate(split(maxima, 3) + split(totals, 3)):
        pick = (src == (lane - group * HEADS) * head_dim) & (lane >= group * HEADS)
        pick = pick & (lane < (group + 1) * HEADS)
        term = dot(part, jnp.where(pick, 1.0, 0.0).astype(BF16))
        stats = term if stats is None else stats + term
    out_ref[:, width:] = stats.astype(BF16)


def unpack(in_ref, width):
    head_dim = width // HEADS
    sums = in_ref[:, :width].astype(F32)
    stats = in_ref[:, width:]
    lane, chan = iota((STATS, width), 0), iota((STATS, width), 1)
    results = [sums]
    for first in (0, 3 * HEADS):
        pick = None
        for group in range(3):
            head = lane - (first + group * HEADS)
            hit = (chan >= head * head_dim) & (chan < (head + 1) * head_dim)
            hit = hit & (head >= 0) & (head < HEADS)
            pick = hit if pick is None else pick | hit
        results.append(dot(stats, jnp.where(pick, 1.0, 0.0).astype(BF16)))
    return results


def combine(parts):
    top = parts[0][1]
    for _, maxima, _ in parts[1:]:
        top = jnp.maximum(top, maxima)
    sums, totals = None, None
    for part_sums, maxima, part_totals in parts:
        scale = jnp.exp(maxima - top)
        s, t = part_sums * scale, part_totals * scale
        sums = s if sums is None else sums + s
        totals = t if totals is None else totals + t
    return sums, top, totals


def kernel(
    sizes, *refs
):
    given, (mem, dec), rest = refs[:9], refs[9:11], refs[11:]
    held, (insem, *rest) = rest[:9], rest[9:]
    loads = {
        name: pltpu.make_async_copy(given[i], held[i], insem.at[i])
        for i, name in enumerate(("feat", "dwk", "gain", "qs", "qp", "wq", "wk", "wv", "wo"))
    }
    for name in ("feat", "qs", "qp", "wq", "dwk", "gain", "wk", "wv", "wo"):
        loads[name].start()
    main(sizes, loads, *held, mem, dec, *rest)


def main(
    sizes, loads, feat, dwk, gain, qs, qp, wq, wk, wv, wo, mem, dec,
    pad, shifted, shift_sel, place_sel, dwf, conv, packed, rowrecv, colrecv, cornrecv, keys, values, qf, queries,
    p1send, p1recv, p2send, p2recv, attended,
    hsend, hrecv, s1, r1, s2, r2, s3, r3,
):
    n_rows, n_cols = sizes["rows"], sizes["cols"]
    n_a, n_b = sizes[SCATTER], sizes[EXCHANGE]
    tile_rows, tile_cols, width = feat.shape
    pixels = tile_rows * tile_cols
    n_query = qs.shape[0]
    block = p2send.shape[0]
    head_dim = width // HEADS
    row, col = lax.axis_index("rows"), lax.axis_index("cols")
    me_a, me_b = lax.axis_index(SCATTER), lax.axis_index(EXCHANGE)

    barrier = pltpu.get_barrier_semaphore()
    for k in range(1, n_a):
        pl.semaphore_signal(
            barrier, inc=1, device_id={SCATTER: lax.rem(me_a + k, n_a)}, device_id_type=MESH
        )
    for k in range(1, n_b):
        pl.semaphore_signal(
            barrier, inc=1, device_id={EXCHANGE: lax.rem(me_b + k, n_b)}, device_id_type=MESH
        )
    for dr, dc in DIRS[4:]:
        pl.semaphore_signal(
            barrier, inc=1,
            device_id={
                "rows": lax.rem(row + dr + n_rows, n_rows),
                "cols": lax.rem(col + dc + n_cols, n_cols),
            },
            device_id_type=MESH,
        )

    loads["feat"].wait()
    flat_in = feat[...].reshape(pixels, width)
    pieces = []
    for first in (0, tile_cols - 3):
        for j in range(3):
            want = iota((tile_rows, pixels), 0) * tile_cols + (first + j)
            pieces.append(want == iota((tile_rows, pixels), 1))
    for dr, dc in DIRS[4:]:
        k = iota((16, pixels), 0)
        i, j = k >> 2, k & 3
        r0 = 0 if dr < 0 else tile_rows - 3
        c0 = 0 if dc < 0 else tile_cols - 3
        want = (r0 + i) * tile_cols + c0 + j
        pieces.append((want == iota((16, pixels), 1)) & (i < 3) & (j < 3))
    select = jnp.concatenate([jnp.where(p, 1.0, 0.0).astype(BF16) for p in pieces], axis=0)
    packed[...] = dot(select, flat_in).astype(BF16)

    pl.semaphore_wait(barrier, (n_a - 1) + (n_b - 1) + 4)

    def halo(index):
        dr, dc = DIRS[index]
        if index < 2:
            src = feat.at[pl.ds(0 if dr < 0 else tile_rows - 3, 3)]
            dst = rowrecv.at[index]
        elif index < 4:
            src = packed.at[pl.ds((index - 2) * 3 * tile_rows, 3 * tile_rows)]
            dst = colrecv.at[index - 2]
        else:
            src = packed.at[pl.ds(6 * tile_rows + (index - 4) * 16, 16)]
            dst = cornrecv.at[index - 4]
        there = (
            (row + dr >= 0) & (row + dr < n_rows) & (col + dc >= 0) & (col + dc < n_cols)
        )
        comes = (
            (row - dr >= 0) & (row - dr < n_rows) & (col - dc >= 0) & (col - dc < n_cols)
        )
        copy = pltpu.make_async_remote_copy(
            src_ref=src, dst_ref=dst, send_sem=hsend.at[index], recv_sem=hrecv.at[index],
            device_id={"rows": row + dr, "cols": col + dc}, device_id_type=MESH,
        )
        return copy, there, comes, dst

    halos = [halo(i) for i in range(8)]
    for index in (2, 3, 4, 5, 6, 7, 0, 1):
        copy, there, comes, dst = halos[index]

        @pl.when(there)
        def _():
            copy.start()

        @pl.when(jnp.logical_not(comes))
        def _():
            dst[...] = jnp.zeros(dst.shape, BF16)

    wide = 2 * tile_cols

    def place(step_q, step_k, shape, j_major):
        q, k = iota(shape, 0), iota(shape, 1)
        half = shape[1] // 2
        is_right = k < half
        k = jnp.where(k >= half, k - half, k)
        if j_major:
            j = jnp.where(k >= step_k, 1, 0) + jnp.where(k >= 2 * step_k, 1, 0)
            r = k - j * step_k
            fits = k >= 0
        else:
            j, r = k & 3, k >> 2
            fits = (j < 3) & (r < 3)
        hit = (q == r * step_q + j + jnp.where(is_right, 0, tile_cols - 3)) & fits
        return jnp.where(hit, 1.0, 0.0).astype(BF16)

    place_sel[...] = place(tile_cols, tile_rows, (pixels, 6 * tile_rows), True)
    corner = place(tile_cols, 0, (3 * tile_cols, 32), False)
    out, src = iota((8 * tile_cols, 8 * wide), 0), iota((8 * tile_cols, 8 * wide), 1)
    out_row, out_col = out // tile_cols, out % tile_cols
    shifts = []
    for dc in range(7):
        at = out_col + dc - 3
        at = jnp.where(at < 0, at + wide, at)
        shifts.append(jnp.where(src == out_row * wide + at, 1.0, 0.0).astype(BF16))
    shift_sel[...] = jnp.concatenate(shifts, axis=0)
    pad[tile_rows + 6 :] = jnp.zeros((pad.shape[0] - tile_rows - 6, wide, width), BF16)

    pad[pl.ds(3, tile_rows), :tile_cols, :] = feat[...]
    loads["dwk"].wait()
    loads["gain"].wait()
    dwf[...] = dwk[...].astype(F32)
    loads["qs"].wait()
    loads["qp"].wait()
    loads["wq"].wait()
    mixed = (qs[...].astype(F32) + qp[...].astype(F32)).astype(BF16)
    qf[...] = jnp.zeros(qf.shape, F32)
    qf[0:n_query, :] = dot(mixed, wq[...]) * head_dim ** (-0.5)
    queries[...] = qf[...].astype(BF16)

    for index in range(8):
        copy, there, comes, dst = halos[index]

        @pl.when(comes)
        def _():
            copy.wait_recv()

    for index in range(2):
        at = 0 if DIRS[index][0] > 0 else tile_rows + 3
        pad[at : at + 3, :tile_cols, :] = rowrecv[index]

    slab = dot(
        place_sel[...],
        colrecv[...].reshape(6 * tile_rows, width),
    ).astype(BF16)
    pad[pl.ds(3, tile_rows), tile_cols:, :] = slab.reshape(tile_rows, tile_cols, width)
    for first, at in ((0, tile_rows + 3), (2, 0)):
        slab = dot(corner, cornrecv[first : first + 2].reshape(32, width)).astype(BF16)
        pad[at : at + 3, tile_cols:, :] = slab.reshape(3, tile_cols, width)

    for group in range(pad.shape[0] // 8):
        moved = dot(shift_sel[...], pad[8 * group : 8 * group + 8].reshape(8 * wide, width))
        shifted[:, 8 * group : 8 * group + 8] = moved.reshape(7, 8, tile_cols, width)

    chunk = 8
    scale = gain[...]

    def conv_chunk(step, carry):
        r0 = step * chunk
        for g in range(tile_cols // 8):
            acc = [jnp.zeros((8, width), F32) for _ in range(chunk)]
            for dc in range(7):
                taps = [
                    jnp.broadcast_to(dwf[dr, dc : dc + 1, :], (8, width)) for dr in range(7)
                ]
                for i in range(chunk + 6):
                    x = shifted[dc, r0 + i, 8 * g : 8 * g + 8, :]
                    for dr in range(7):
                        o = i - dr
                        if 0 <= o < chunk:
                            acc[o] = acc[o] + x * taps[dr]
            for o in range(chunk):
                conv[o, 8 * g : 8 * g + 8, :] = acc[o]
        normed = layer_norm(conv[...].reshape(chunk * tile_cols, width))
        image = feat[pl.ds(r0, chunk)].astype(F32).reshape(chunk * tile_cols, width)
        result = (image + normed * scale).astype(BF16)
        mem[pl.ds(r0, chunk)] = result.reshape(chunk, tile_cols, width)
        return carry

    lax.fori_loop(0, tile_rows // chunk, conv_chunk, 0)

    loads["wk"].wait()
    loads["wv"].wait()
    flat = mem[...].reshape(pixels, width)
    keys[...] = dot(flat, wk[...]).astype(BF16)
    values[...] = dot(flat, wv[...]).astype(BF16)

    def attend(index):
        q = queries[pl.ds(pl.multiple_of(index * block, 16), block), :]
        head_of = iota((block, width), 1) // head_dim
        spread = jnp.concatenate(
            [jnp.where(head_of == h, q, jnp.zeros_like(q)) for h in range(HEADS)], axis=0
        )
        scores = lax.dot_general(
            spread, keys[...], (((1,), (1,)), ((), ())), preferred_element_type=F32
        )
        top = jnp.max(scores, axis=-1, keepdims=True)
        expo = jnp.exp(scores - top)
        total = jnp.sum(expo, axis=-1, keepdims=True)
        out = dot(expo.astype(BF16), values[...])
        sums = jnp.zeros((block, width), F32)
        maxima = jnp.zeros((block, width), F32)
        totals = jnp.zeros((block, width), F32)
        for h in range(HEADS):
            rows = slice(h * block, (h + 1) * block)
            here = head_of == h
            sums = jnp.where(here, out[rows], sums)
            maxima = jnp.where(here, top[rows], maxima)
            totals = jnp.where(here, total[rows], totals)
        return sums, maxima, totals

    def p1(k):
        return pltpu.make_async_remote_copy(
            src_ref=p1send.at[k - 1], dst_ref=p1recv.at[k - 1],
            send_sem=s1.at[k - 1], recv_sem=r1.at[k - 1],
            device_id={SCATTER: lax.rem(me_a + k, n_a)}, device_id_type=MESH,
        )

    def scatter_step(step, carry):
        k = step + 1
        pack(p1send.at[step], *attend(lax.rem(me_a + k, n_a)))
        p1(k).start()
        return carry

    lax.fori_loop(0, n_a - 1, scatter_step, 0)
    parts = [attend(me_a)]
    for k in range(1, n_a):
        p1(k).wait_recv()
        parts.append(unpack(p1recv.at[k - 1], width))
    mine = combine(parts)
    pack(p2send, *mine)

    def p2(k):
        return pltpu.make_async_remote_copy(
            src_ref=p2send, dst_ref=p2recv.at[k - 1],
            send_sem=s2.at[k - 1], recv_sem=r2.at[k - 1],
            device_id={EXCHANGE: lax.rem(me_b + k, n_b)}, device_id_type=MESH,
        )

    for k in range(1, n_b):
        p2(k).start()
    parts = [unpack(p2send, width)]
    for k in range(1, n_b):
        p2(k).wait_recv()
        parts.append(unpack(p2recv.at[k - 1], width))
    sums, _, totals = combine(parts)
    attended[me_a] = (sums / totals).astype(BF16)

    def p3(k):
        return pltpu.make_async_remote_copy(
            src_ref=attended.at[me_a], dst_ref=attended.at[me_a],
            send_sem=s3.at[k - 1], recv_sem=r3.at[k - 1],
            device_id={SCATTER: lax.rem(me_a + k, n_a)}, device_id_type=MESH,
        )

    for k in range(1, n_a):
        p3(k).start()
    for k in range(1, n_a):
        p3(k).wait_recv()
    loads["wo"].wait()
    projected = dot(attended[...].reshape(n_a * block, width), wo[...])
    dec[...] = layer_norm(qs[...].astype(F32) + projected[:n_query])

    for index in range(8):
        copy, there, comes, dst = halos[index]

        @pl.when(there)
        def _():
            copy.wait_send()

    for k in range(1, n_a):
        p1(k).wait_send()
        p3(k).wait_send()
    for k in range(1, n_b):
        p2(k).wait_send()


def body(sizes, features, dw_kernel, norm_gain, query_state, query_pos, wq, wk, wv, wo):
    tile_rows, tile_cols, width = features.shape
    n_query = query_state.shape[0]
    n_a, n_b = sizes[SCATTER], sizes[EXCHANGE]
    block = -(-n_query // (16 * n_a)) * 16
    pixels = tile_rows * tile_cols
    row_bytes = width + STATS
    vmem = pl.BlockSpec(memory_space=pltpu.VMEM)
    dma = pltpu.SemaphoreType.DMA
    given = (
        features, dw_kernel, norm_gain.reshape(1, width), query_state, query_pos, wq, wk, wv, wo
    )
    return pl.pallas_call(
        functools.partial(kernel, sizes),
        out_shape=(
            jax.ShapeDtypeStruct(features.shape, BF16),
            jax.ShapeDtypeStruct((n_query, width), F32),
        ),
        in_specs=[pl.BlockSpec(memory_space=pltpu.HBM)] * 9,
        out_specs=(vmem, vmem),
        scratch_shapes=[pltpu.VMEM(x.shape, x.dtype) for x in given] + [
            dma((9,)),
            pltpu.VMEM((tile_rows + 8, 2 * tile_cols, width), BF16),
            pltpu.VMEM((7, tile_rows + 8, tile_cols, width), F32),
            pltpu.VMEM((7 * 8 * tile_cols, 16 * tile_cols), BF16),
            pltpu.VMEM((pixels, 6 * tile_rows), BF16),
            pltpu.VMEM((7, 7, width), F32),
            pltpu.VMEM((8, tile_cols, width), F32),
            pltpu.VMEM((6 * tile_rows + 64, width), BF16),
            pltpu.VMEM((2, 3, tile_cols, width), BF16),
            pltpu.VMEM((2, 3 * tile_rows, width), BF16),
            pltpu.VMEM((4, 16, width), BF16),
            pltpu.VMEM((pixels, width), BF16),
            pltpu.VMEM((pixels, width), BF16),
            pltpu.VMEM((n_a * block, width), F32),
            pltpu.VMEM((n_a * block, width), BF16),
            pltpu.VMEM((n_a - 1, block, row_bytes), BF16),
            pltpu.VMEM((n_a - 1, block, row_bytes), BF16),
            pltpu.VMEM((block, row_bytes), BF16),
            pltpu.VMEM((n_b - 1, block, row_bytes), BF16),
            pltpu.VMEM((n_a, block, width), BF16),
            dma((8,)), dma((8,)),
            dma((n_a - 1,)), dma((n_a - 1,)),
            dma((n_b - 1,)), dma((n_b - 1,)),
            dma((n_a - 1,)), dma((n_a - 1,)),
        ],
        compiler_params=pltpu.CompilerParams(
            collective_id=0, has_side_effects=True, vmem_limit_bytes=62 * 1024 * 1024
        ),
    )(*given)


def solution(mesh):
    sizes = dict(mesh.shape)
    in_specs = (
        P(("scenes", "rows"), "cols", None),
        P(),
        P(),
        P("scenes", None),
        P("scenes", None),
        P(),
        P(),
        P(),
        P(),
    )
    out_specs = (P(("scenes", "rows"), "cols", None), P("scenes", None))
    return jax.shard_map(
        functools.partial(body, sizes), mesh=mesh, in_specs=in_specs, out_specs=out_specs,
        check_vma=False,
    )
```

```python
import functools
import jax
import jax.numpy as jnp
from jax import lax
from jax.experimental import pallas as pl
from jax.experimental.pallas import tpu as pltpu
from jax.sharding import PartitionSpec as P

HEADS = 8
SCATTER = "rows"
EXCHANGE = "cols"
MESH = pl.DeviceIdType.MESH
F32 = jnp.float32
BF16 = jnp.bfloat16
TERMS = 6
FOLD = 5

DIRS = ((-1, 0), (1, 0), (0, -1), (0, 1), (-1, -1), (-1, 1), (1, -1), (1, 1))


def iota(shape, dim):
    return lax.broadcasted_iota(jnp.int32, shape, dim)


def layer_norm(vector):
    centred = vector - jnp.mean(vector, axis=-1, keepdims=True)
    variance = jnp.mean(centred * centred, axis=-1, keepdims=True)
    return centred * lax.rsqrt(variance + 1e-06)


def dot(a, b):
    return jnp.dot(a, b, preferred_element_type=F32)


def split(value, terms):
    parts = []
    for _ in range(terms):
        part = value.astype(BF16)
        parts.append(part)
        value = value - part.astype(F32)
    return parts


def stat_rows(block):
    return -(-block // (16 * FOLD)) * 16


def make_picks(to_stats, to_wide):
    width = to_stats.shape[1]
    head_dim = width // HEADS
    src, lane = iota((width, width), 0), iota((width, width), 1)
    for group in range(TERMS):
        head = lane - group * HEADS
        hit = (src == head * head_dim) & (head >= 0) & (head < HEADS)
        to_stats[group] = jnp.where(hit, 1.0, 0.0).astype(BF16)
    for which in range(2):
        pick = None
        for group in range(3 * which, 3 * which + 3):
            head = src - group * HEADS
            hit = (lane >= head * head_dim) & (lane < (head + 1) * head_dim)
            hit = hit & (head >= 0) & (head < HEADS)
            pick = hit if pick is None else pick | hit
        to_wide[which] = jnp.where(pick, 1.0, 0.0).astype(BF16)


def pack(to_stats, out_ref, sums, maxima, totals):
    block, width = sums.shape
    out_ref[:block] = sums.astype(BF16)
    stats = None
    for group, part in enumerate(split(maxima, 3) + split(totals, 3)):
        term = dot(part, to_stats[group])
        stats = term if stats is None else stats + term
    span = TERMS * HEADS
    for first in range(0, block // 16, FOLD):
        folded = None
        for t in range(first, min(first + FOLD, block // 16)):
            part = stats[16 * t : 16 * t + 16]
            if t > first:
                part = pltpu.roll(part, span * (t - first), 1)
            folded = part if folded is None else folded + part
        at = block + 16 * (first // FOLD)
        out_ref[at : at + 16] = folded.astype(BF16)


def unpack(to_wide, in_ref, block):
    width = in_ref.shape[1]
    sums = in_ref[:block].astype(F32)
    span = TERMS * HEADS
    rows = []
    for t in range(block // 16):
        at = block + 16 * (t // FOLD)
        part = in_ref[at : at + 16].astype(F32)
        if t % FOLD:
            part = pltpu.roll(part, width - span * (t % FOLD), 1)
        rows.append(part)
    stats = jnp.concatenate(rows, axis=0).astype(BF16)
    return sums, dot(stats, to_wide[0]), dot(stats, to_wide[1])


def combine(parts):
    top = parts[0][1]
    for _, maxima, _ in parts[1:]:
        top = jnp.maximum(top, maxima)
    sums, totals = None, None
    for part_sums, maxima, part_totals in parts:
        scale = jnp.exp(maxima - top)
        s, t = part_sums * scale, part_totals * scale
        sums = s if sums is None else sums + s
        totals = t if totals is None else totals + t
    return sums, top, totals


def kernel(
    sizes, *refs
):
    given, (mem, dec), rest = refs[:9], refs[9:11], refs[11:]
    held, (insem, *rest) = rest[:9], rest[9:]
    loads = {
        name: pltpu.make_async_copy(given[i], held[i], insem.at[i])
        for i, name in enumerate(("feat", "dwk", "gain", "qs", "qp", "wq", "wk", "wv", "wo"))
    }
    for name in ("feat", "qs", "qp", "wq", "dwk", "gain", "wk", "wv", "wo"):
        loads[name].start()
    main(sizes, loads, *held, mem, dec, *rest)


def main(
    sizes, loads, feat, dwk, gain, qs, qp, wq, wk, wv, wo, mem, dec,
    to_stats, to_wide, pad, shifted, shift_sel, place_sel, dwf, conv, packed, rowrecv, colrecv, cornrecv, keys, values, qf, queries,
    p1send, p1recv, p2send, p2recv, attended,
    hsend, hrecv, s1, r1, s2, r2, s3, r3,
):
    n_rows, n_cols = sizes["rows"], sizes["cols"]
    n_a, n_b = sizes[SCATTER], sizes[EXCHANGE]
    tile_rows, tile_cols, width = feat.shape
    pixels = tile_rows * tile_cols
    n_query = qs.shape[0]
    block = attended.shape[1]
    head_dim = width // HEADS
    row, col = lax.axis_index("rows"), lax.axis_index("cols")
    me_a, me_b = lax.axis_index(SCATTER), lax.axis_index(EXCHANGE)

    barrier = pltpu.get_barrier_semaphore()
    for k in range(1, n_a):
        pl.semaphore_signal(
            barrier, inc=1, device_id={SCATTER: lax.rem(me_a + k, n_a)}, device_id_type=MESH
        )
    for k in range(1, n_b):
        pl.semaphore_signal(
            barrier, inc=1, device_id={EXCHANGE: lax.rem(me_b + k, n_b)}, device_id_type=MESH
        )
    for dr, dc in DIRS[4:]:
        pl.semaphore_signal(
            barrier, inc=1,
            device_id={
                "rows": lax.rem(row + dr + n_rows, n_rows),
                "cols": lax.rem(col + dc + n_cols, n_cols),
            },
            device_id_type=MESH,
        )

    loads["feat"].wait()
    flat_in = feat[...].reshape(pixels, width)
    pieces = []
    for first in (0, tile_cols - 3):
        for j in range(3):
            want = iota((tile_rows, pixels), 0) * tile_cols + (first + j)
            pieces.append(want == iota((tile_rows, pixels), 1))
    for dr, dc in DIRS[4:]:
        k = iota((16, pixels), 0)
        i, j = k >> 2, k & 3
        r0 = 0 if dr < 0 else tile_rows - 3
        c0 = 0 if dc < 0 else tile_cols - 3
        want = (r0 + i) * tile_cols + c0 + j
        pieces.append((want == iota((16, pixels), 1)) & (i < 3) & (j < 3))
    select = jnp.concatenate([jnp.where(p, 1.0, 0.0).astype(BF16) for p in pieces], axis=0)
    packed[...] = dot(select, flat_in).astype(BF16)

    pl.semaphore_wait(barrier, (n_a - 1) + (n_b - 1) + 4)

    def halo(index):
        dr, dc = DIRS[index]
        if index < 2:
            src = feat.at[pl.ds(0 if dr < 0 else tile_rows - 3, 3)]
            dst = rowrecv.at[index]
        elif index < 4:
            src = packed.at[pl.ds((index - 2) * 3 * tile_rows, 3 * tile_rows)]
            dst = colrecv.at[index - 2]
        else:
            src = packed.at[pl.ds(6 * tile_rows + (index - 4) * 16, 16)]
            dst = cornrecv.at[index - 4]
        there = (
            (row + dr >= 0) & (row + dr < n_rows) & (col + dc >= 0) & (col + dc < n_cols)
        )
        comes = (
            (row - dr >= 0) & (row - dr < n_rows) & (col - dc >= 0) & (col - dc < n_cols)
        )
        copy = pltpu.make_async_remote_copy(
            src_ref=src, dst_ref=dst, send_sem=hsend.at[index], recv_sem=hrecv.at[index],
            device_id={"rows": row + dr, "cols": col + dc}, device_id_type=MESH,
        )
        return copy, there, comes, dst

    halos = [halo(i) for i in range(8)]
    for index in (2, 3, 4, 5, 6, 7, 0, 1):
        copy, there, comes, dst = halos[index]

        @pl.when(there)
        def _():
            copy.start()

        @pl.when(jnp.logical_not(comes))
        def _():
            dst[...] = jnp.zeros(dst.shape, BF16)

    make_picks(to_stats, to_wide)
    wide = 2 * tile_cols

    def place(step_q, step_k, shape, j_major):
        q, k = iota(shape, 0), iota(shape, 1)
        half = shape[1] // 2
        is_right = k < half
        k = jnp.where(k >= half, k - half, k)
        if j_major:
            j = jnp.where(k >= step_k, 1, 0) + jnp.where(k >= 2 * step_k, 1, 0)
            r = k - j * step_k
            fits = k >= 0
        else:
            j, r = k & 3, k >> 2
            fits = (j < 3) & (r < 3)
        hit = (q == r * step_q + j + jnp.where(is_right, 0, tile_cols - 3)) & fits
        return jnp.where(hit, 1.0, 0.0).astype(BF16)

    place_sel[...] = place(tile_cols, tile_rows, (pixels, 6 * tile_rows), True)
    corner = place(tile_cols, 0, (3 * tile_cols, 32), False)
    out, src = iota((8 * tile_cols, 8 * wide), 0), iota((8 * tile_cols, 8 * wide), 1)
    out_row, out_col = out // tile_cols, out % tile_cols
    shifts = []
    for dc in range(7):
        at = out_col + dc - 3
        at = jnp.where(at < 0, at + wide, at)
        shifts.append(jnp.where(src == out_row * wide + at, 1.0, 0.0).astype(BF16))
    shift_sel[...] = jnp.concatenate(shifts, axis=0)
    pad[tile_rows + 6 :] = jnp.zeros((pad.shape[0] - tile_rows - 6, wide, width), BF16)

    pad[pl.ds(3, tile_rows), :tile_cols, :] = feat[...]
    loads["dwk"].wait()
    loads["gain"].wait()
    dwf[...] = dwk[...].astype(F32)
    loads["qs"].wait()
    loads["qp"].wait()
    loads["wq"].wait()
    mixed = (qs[...].astype(F32) + qp[...].astype(F32)).astype(BF16)
    qf[...] = jnp.zeros(qf.shape, F32)
    qf[0:n_query, :] = dot(mixed, wq[...]) * head_dim ** (-0.5)
    queries[...] = qf[...].astype(BF16)

    for index in range(8):
        copy, there, comes, dst = halos[index]

        @pl.when(comes)
        def _():
            copy.wait_recv()

    for index in range(2):
        at = 0 if DIRS[index][0] > 0 else tile_rows + 3
        pad[at : at + 3, :tile_cols, :] = rowrecv[index]

    slab = dot(
        place_sel[...],
        colrecv[...].reshape(6 * tile_rows, width),
    ).astype(BF16)
    pad[pl.ds(3, tile_rows), tile_cols:, :] = slab.reshape(tile_rows, tile_cols, width)
    for first, at in ((0, tile_rows + 3), (2, 0)):
        slab = dot(corner, cornrecv[first : first + 2].reshape(32, width)).astype(BF16)
        pad[at : at + 3, tile_cols:, :] = slab.reshape(3, tile_cols, width)

    for group in range(pad.shape[0] // 8):
        moved = dot(shift_sel[...], pad[8 * group : 8 * group + 8].reshape(8 * wide, width))
        shifted[:, 8 * group : 8 * group + 8] = moved.reshape(7, 8, tile_cols, width)

    chunk = 8
    scale = gain[...]

    def conv_chunk(step, carry):
        r0 = step * chunk
        for g in range(tile_cols // 8):
            acc = [jnp.zeros((8, width), F32) for _ in range(chunk)]
            for dc in range(7):
                taps = [
                    jnp.broadcast_to(dwf[dr, dc : dc + 1, :], (8, width)) for dr in range(7)
                ]
                for i in range(chunk + 6):
                    x = shifted[dc, r0 + i, 8 * g : 8 * g + 8, :]
                    for dr in range(7):
                        o = i - dr
                        if 0 <= o < chunk:
                            acc[o] = acc[o] + x * taps[dr]
            for o in range(chunk):
                conv[o, 8 * g : 8 * g + 8, :] = acc[o]
        normed = layer_norm(conv[...].reshape(chunk * tile_cols, width))
        image = feat[pl.ds(r0, chunk)].astype(F32).reshape(chunk * tile_cols, width)
        result = (image + normed * scale).astype(BF16)
        mem[pl.ds(r0, chunk)] = result.reshape(chunk, tile_cols, width)
        return carry

    lax.fori_loop(0, tile_rows // chunk, conv_chunk, 0)

    loads["wk"].wait()
    loads["wv"].wait()
    flat = mem[...].reshape(pixels, width)
    keys[...] = dot(flat, wk[...]).astype(BF16)
    values[...] = dot(flat, wv[...]).astype(BF16)

    def attend(index):
        q = queries[pl.ds(pl.multiple_of(index * block, 16), block), :]
        head_of = iota((block, width), 1) // head_dim
        spread = jnp.concatenate(
            [jnp.where(head_of == h, q, jnp.zeros_like(q)) for h in range(HEADS)], axis=0
        )
        scores = lax.dot_general(
            spread, keys[...], (((1,), (1,)), ((), ())), preferred_element_type=F32
        )
        top = jnp.max(scores, axis=-1, keepdims=True)
        expo = jnp.exp(scores - top)
        total = jnp.sum(expo, axis=-1, keepdims=True)
        out = dot(expo.astype(BF16), values[...])
        sums = jnp.zeros((block, width), F32)
        maxima = jnp.zeros((block, width), F32)
        totals = jnp.zeros((block, width), F32)
        for h in range(HEADS):
            rows = slice(h * block, (h + 1) * block)
            here = head_of == h
            sums = jnp.where(here, out[rows], sums)
            maxima = jnp.where(here, top[rows], maxima)
            totals = jnp.where(here, total[rows], totals)
        return sums, maxima, totals

    def p1(k):
        return pltpu.make_async_remote_copy(
            src_ref=p1send.at[k - 1], dst_ref=p1recv.at[k - 1],
            send_sem=s1.at[k - 1], recv_sem=r1.at[k - 1],
            device_id={SCATTER: lax.rem(me_a + k, n_a)}, device_id_type=MESH,
        )

    def scatter_step(step, carry):
        k = step + 1
        pack(to_stats, p1send.at[step], *attend(lax.rem(me_a + k, n_a)))
        p1(k).start()
        return carry

    lax.fori_loop(0, n_a - 1, scatter_step, 0)
    parts = [attend(me_a)]
    for k in range(1, n_a):
        p1(k).wait_recv()
        parts.append(unpack(to_wide, p1recv.at[k - 1], block))
    mine = combine(parts)
    pack(to_stats, p2send, *mine)

    def p2(k):
        return pltpu.make_async_remote_copy(
            src_ref=p2send, dst_ref=p2recv.at[k - 1],
            send_sem=s2.at[k - 1], recv_sem=r2.at[k - 1],
            device_id={EXCHANGE: lax.rem(me_b + k, n_b)}, device_id_type=MESH,
        )

    for k in range(1, n_b):
        p2(k).start()
    parts = [unpack(to_wide, p2send, block)]
    for k in range(1, n_b):
        p2(k).wait_recv()
        parts.append(unpack(to_wide, p2recv.at[k - 1], block))
    sums, _, totals = combine(parts)
    attended[me_a] = (sums / totals).astype(BF16)

    def p3(k):
        return pltpu.make_async_remote_copy(
            src_ref=attended.at[me_a], dst_ref=attended.at[me_a],
            send_sem=s3.at[k - 1], recv_sem=r3.at[k - 1],
            device_id={SCATTER: lax.rem(me_a + k, n_a)}, device_id_type=MESH,
        )

    for k in range(1, n_a):
        p3(k).start()
    for k in range(1, n_a):
        p3(k).wait_recv()
    loads["wo"].wait()
    projected = dot(attended[...].reshape(n_a * block, width), wo[...])
    dec[...] = layer_norm(qs[...].astype(F32) + projected[:n_query])

    for index in range(8):
        copy, there, comes, dst = halos[index]

        @pl.when(there)
        def _():
            copy.wait_send()

    for k in range(1, n_a):
        p1(k).wait_send()
        p3(k).wait_send()
    for k in range(1, n_b):
        p2(k).wait_send()


def body(sizes, features, dw_kernel, norm_gain, query_state, query_pos, wq, wk, wv, wo):
    tile_rows, tile_cols, width = features.shape
    n_query = query_state.shape[0]
    n_a, n_b = sizes[SCATTER], sizes[EXCHANGE]
    block = -(-n_query // (16 * n_a)) * 16
    pixels = tile_rows * tile_cols
    message = block + stat_rows(block)
    vmem = pl.BlockSpec(memory_space=pltpu.VMEM)
    dma = pltpu.SemaphoreType.DMA
    given = (
        features, dw_kernel, norm_gain.reshape(1, width), query_state, query_pos, wq, wk, wv, wo
    )
    return pl.pallas_call(
        functools.partial(kernel, sizes),
        out_shape=(
            jax.ShapeDtypeStruct(features.shape, BF16),
            jax.ShapeDtypeStruct((n_query, width), F32),
        ),
        in_specs=[pl.BlockSpec(memory_space=pltpu.HBM)] * 9,
        out_specs=(vmem, vmem),
        scratch_shapes=[pltpu.VMEM(x.shape, x.dtype) for x in given] + [
            dma((9,)),
            pltpu.VMEM((TERMS, width, width), BF16),
            pltpu.VMEM((2, width, width), BF16),
            pltpu.VMEM((tile_rows + 8, 2 * tile_cols, width), BF16),
            pltpu.VMEM((7, tile_rows + 8, tile_cols, width), F32),
            pltpu.VMEM((7 * 8 * tile_cols, 16 * tile_cols), BF16),
            pltpu.VMEM((pixels, 6 * tile_rows), BF16),
            pltpu.VMEM((7, 7, width), F32),
            pltpu.VMEM((8, tile_cols, width), F32),
            pltpu.VMEM((6 * tile_rows + 64, width), BF16),
            pltpu.VMEM((2, 3, tile_cols, width), BF16),
            pltpu.VMEM((2, 3 * tile_rows, width), BF16),
            pltpu.VMEM((4, 16, width), BF16),
            pltpu.VMEM((pixels, width), BF16),
            pltpu.VMEM((pixels, width), BF16),
            pltpu.VMEM((n_a * block, width), F32),
            pltpu.VMEM((n_a * block, width), BF16),
            pltpu.VMEM((n_a - 1, message, width), BF16),
            pltpu.VMEM((n_a - 1, message, width), BF16),
            pltpu.VMEM((message, width), BF16),
            pltpu.VMEM((n_b - 1, message, width), BF16),
            pltpu.VMEM((n_a, block, width), BF16),
            dma((8,)), dma((8,)),
            dma((n_a - 1,)), dma((n_a - 1,)),
            dma((n_b - 1,)), dma((n_b - 1,)),
            dma((n_a - 1,)), dma((n_a - 1,)),
        ],
        compiler_params=pltpu.CompilerParams(
            collective_id=0, has_side_effects=True, vmem_limit_bytes=62 * 1024 * 1024
        ),
    )(*given)


def solution(mesh):
    sizes = dict(mesh.shape)
    in_specs = (
        P(("scenes", "rows"), "cols", None),
        P(),
        P(),
        P("scenes", None),
        P("scenes", None),
        P(),
        P(),
        P(),
        P(),
    )
    out_specs = (P(("scenes", "rows"), "cols", None), P("scenes", None))
    return jax.shard_map(
        functools.partial(body, sizes), mesh=mesh, in_specs=in_specs, out_specs=out_specs,
        check_vma=False,
    )
```

```python
import functools
import jax
import jax.numpy as jnp
from jax import lax
from jax.experimental import pallas as pl
from jax.experimental.pallas import tpu as pltpu
from jax.sharding import PartitionSpec as P

HEADS = 8
SCATTER = "rows"
EXCHANGE = "cols"
MESH = pl.DeviceIdType.MESH
F32 = jnp.float32
BF16 = jnp.bfloat16
TERMS = 6
FOLD = 5

DIRS = ((-1, 0), (1, 0), (0, -1), (0, 1), (-1, -1), (-1, 1), (1, -1), (1, 1))


def iota(shape, dim):
    return lax.broadcasted_iota(jnp.int32, shape, dim)


def layer_norm(vector):
    centred = vector - jnp.mean(vector, axis=-1, keepdims=True)
    variance = jnp.mean(centred * centred, axis=-1, keepdims=True)
    return centred * lax.rsqrt(variance + 1e-06)


def dot(a, b):
    return jnp.dot(a, b, preferred_element_type=F32)


def split(value, terms):
    parts = []
    for _ in range(terms):
        part = value.astype(BF16)
        parts.append(part)
        value = value - part.astype(F32)
    return parts


def stat_rows(block):
    return -(-block // (16 * FOLD)) * 16


def make_picks(to_stats, to_wide):
    width = to_stats.shape[1]
    head_dim = width // HEADS
    src, lane = iota((width, width), 0), iota((width, width), 1)
    for group in range(TERMS):
        head = lane - group * HEADS
        hit = (src == head * head_dim) & (head >= 0) & (head < HEADS)
        to_stats[group] = jnp.where(hit, 1.0, 0.0).astype(BF16)
    for which in range(2):
        pick = None
        for group in range(3 * which, 3 * which + 3):
            head = src - group * HEADS
            hit = (lane >= head * head_dim) & (lane < (head + 1) * head_dim)
            hit = hit & (head >= 0) & (head < HEADS)
            pick = hit if pick is None else pick | hit
        to_wide[which] = jnp.where(pick, 1.0, 0.0).astype(BF16)


def pack(to_stats, out_ref, sums, maxima, totals):
    block, width = sums.shape
    out_ref[:block] = sums.astype(BF16)
    stats = None
    for group, part in enumerate(split(maxima, 3) + split(totals, 3)):
        term = dot(part, to_stats[group])
        stats = term if stats is None else stats + term
    span = TERMS * HEADS
    for first in range(0, block // 16, FOLD):
        folded = None
        for t in range(first, min(first + FOLD, block // 16)):
            part = stats[16 * t : 16 * t + 16]
            if t > first:
                part = pltpu.roll(part, span * (t - first), 1)
            folded = part if folded is None else folded + part
        at = block + 16 * (first // FOLD)
        out_ref[at : at + 16] = folded.astype(BF16)


def unpack(to_wide, in_ref, block):
    width = in_ref.shape[1]
    sums = in_ref[:block].astype(F32)
    span = TERMS * HEADS
    rows = []
    for t in range(block // 16):
        at = block + 16 * (t // FOLD)
        part = in_ref[at : at + 16].astype(F32)
        if t % FOLD:
            part = pltpu.roll(part, width - span * (t % FOLD), 1)
        rows.append(part)
    stats = jnp.concatenate(rows, axis=0).astype(BF16)
    return sums, dot(stats, to_wide[0]), dot(stats, to_wide[1])


def combine(parts):
    top = parts[0][1]
    for _, maxima, _ in parts[1:]:
        top = jnp.maximum(top, maxima)
    sums, totals = None, None
    for part_sums, maxima, part_totals in parts:
        scale = jnp.exp(maxima - top)
        s, t = part_sums * scale, part_totals * scale
        sums = s if sums is None else sums + s
        totals = t if totals is None else totals + t
    return sums, top, totals


def kernel(
    sizes, *refs
):
    given, (mem, dec), rest = refs[:9], refs[9:11], refs[11:]
    held, (insem, *rest) = rest[:9], rest[9:]
    loads = {
        name: pltpu.make_async_copy(given[i], held[i], insem.at[i])
        for i, name in enumerate(("feat", "dwk", "gain", "qs", "qp", "wq", "wk", "wv", "wo"))
    }
    for name in ("feat", "qs", "qp", "wq", "dwk", "gain", "wk", "wv", "wo"):
        loads[name].start()
    main(sizes, loads, *held, mem, dec, *rest)


def main(
    sizes, loads, feat, dwk, gain, qs, qp, wq, wk, wv, wo, mem, dec,
    to_stats, to_wide, pad, shifted, shift_sel, place_sel, dwf, conv, packed, rowrecv, colrecv, cornrecv, keys, values, qf, queries,
    p1send, p1recv, p2send, p2recv, attended,
    hsend, hrecv, s1, r1, s2, r2, s3, r3,
):
    n_rows, n_cols = sizes["rows"], sizes["cols"]
    n_a, n_b = sizes[SCATTER], sizes[EXCHANGE]
    tile_rows, tile_cols, width = feat.shape
    pixels = tile_rows * tile_cols
    n_query = qs.shape[0]
    block = attended.shape[1]
    head_dim = width // HEADS
    row, col = lax.axis_index("rows"), lax.axis_index("cols")
    me_a, me_b = lax.axis_index(SCATTER), lax.axis_index(EXCHANGE)

    barrier = pltpu.get_barrier_semaphore()
    for k in range(1, n_a):
        pl.semaphore_signal(
            barrier, inc=1, device_id={SCATTER: lax.rem(me_a + k, n_a)}, device_id_type=MESH
        )
    for k in range(1, n_b):
        pl.semaphore_signal(
            barrier, inc=1, device_id={EXCHANGE: lax.rem(me_b + k, n_b)}, device_id_type=MESH
        )
    for dr, dc in DIRS[4:]:
        pl.semaphore_signal(
            barrier, inc=1,
            device_id={
                "rows": lax.rem(row + dr + n_rows, n_rows),
                "cols": lax.rem(col + dc + n_cols, n_cols),
            },
            device_id_type=MESH,
        )

    loads["feat"].wait()
    flat_in = feat[...].reshape(pixels, width)
    pieces = []
    for first in (0, tile_cols - 3):
        for j in range(3):
            want = iota((tile_rows, pixels), 0) * tile_cols + (first + j)
            pieces.append(want == iota((tile_rows, pixels), 1))
    for dr, dc in DIRS[4:]:
        k = iota((16, pixels), 0)
        i, j = k >> 2, k & 3
        r0 = 0 if dr < 0 else tile_rows - 3
        c0 = 0 if dc < 0 else tile_cols - 3
        want = (r0 + i) * tile_cols + c0 + j
        pieces.append((want == iota((16, pixels), 1)) & (i < 3) & (j < 3))
    select = jnp.concatenate([jnp.where(p, 1.0, 0.0).astype(BF16) for p in pieces], axis=0)
    packed[...] = dot(select, flat_in).astype(BF16)

    pl.semaphore_wait(barrier, (n_a - 1) + (n_b - 1) + 4)

    def halo(index):
        dr, dc = DIRS[index]
        if index < 2:
            src = feat.at[pl.ds(0 if dr < 0 else tile_rows - 3, 3)]
            dst = rowrecv.at[index]
        elif index < 4:
            src = packed.at[pl.ds((index - 2) * 3 * tile_rows, 3 * tile_rows)]
            dst = colrecv.at[index - 2]
        else:
            src = packed.at[pl.ds(6 * tile_rows + (index - 4) * 16, 16)]
            dst = cornrecv.at[index - 4]
        there = (
            (row + dr >= 0) & (row + dr < n_rows) & (col + dc >= 0) & (col + dc < n_cols)
        )
        comes = (
            (row - dr >= 0) & (row - dr < n_rows) & (col - dc >= 0) & (col - dc < n_cols)
        )
        copy = pltpu.make_async_remote_copy(
            src_ref=src, dst_ref=dst, send_sem=hsend.at[index], recv_sem=hrecv.at[index],
            device_id={"rows": row + dr, "cols": col + dc}, device_id_type=MESH,
        )
        return copy, there, comes, dst

    halos = [halo(i) for i in range(8)]
    for index in (2, 3, 4, 5, 6, 7, 0, 1):
        copy, there, comes, dst = halos[index]

        @pl.when(there)
        def _():
            copy.start()

        @pl.when(jnp.logical_not(comes))
        def _():
            dst[...] = jnp.zeros(dst.shape, BF16)

    make_picks(to_stats, to_wide)
    wide = 2 * tile_cols

    def place(step_q, step_k, shape, j_major):
        q, k = iota(shape, 0), iota(shape, 1)
        half = shape[1] // 2
        is_right = k < half
        k = jnp.where(k >= half, k - half, k)
        if j_major:
            j = jnp.where(k >= step_k, 1, 0) + jnp.where(k >= 2 * step_k, 1, 0)
            r = k - j * step_k
            fits = k >= 0
        else:
            j, r = k & 3, k >> 2
            fits = (j < 3) & (r < 3)
        hit = (q == r * step_q + j + jnp.where(is_right, 0, tile_cols - 3)) & fits
        return jnp.where(hit, 1.0, 0.0).astype(BF16)

    place_sel[...] = place(tile_cols, tile_rows, (pixels, 6 * tile_rows), True)
    corner = place(tile_cols, 0, (3 * tile_cols, 32), False)
    out, src = iota((8 * tile_cols, 8 * wide), 0), iota((8 * tile_cols, 8 * wide), 1)
    out_row, out_col = out // tile_cols, out % tile_cols
    shifts = []
    for dc in range(7):
        at = out_col + dc - 3
        at = jnp.where(at < 0, at + wide, at)
        shifts.append(jnp.where(src == out_row * wide + at, 1.0, 0.0).astype(BF16))
    shift_sel[...] = jnp.concatenate(shifts, axis=0)
    pad[tile_rows + 6 :] = jnp.zeros((pad.shape[0] - tile_rows - 6, wide, width), BF16)

    pad[pl.ds(3, tile_rows), :tile_cols, :] = feat[...]
    loads["dwk"].wait()
    loads["gain"].wait()
    dwf[...] = dwk[...].astype(F32)
    loads["qs"].wait()
    loads["qp"].wait()
    loads["wq"].wait()
    mixed = (qs[...].astype(F32) + qp[...].astype(F32)).astype(BF16)
    qf[...] = jnp.zeros(qf.shape, F32)
    qf[0:n_query, :] = dot(mixed, wq[...]) * head_dim ** (-0.5)
    queries[...] = qf[...].astype(BF16)

    for index in range(8):
        copy, there, comes, dst = halos[index]

        @pl.when(comes)
        def _():
            copy.wait_recv()

    for index in range(2):
        at = 0 if DIRS[index][0] > 0 else tile_rows + 3
        pad[at : at + 3, :tile_cols, :] = rowrecv[index]

    slab = dot(
        place_sel[...],
        colrecv[...].reshape(6 * tile_rows, width),
    ).astype(BF16)
    pad[pl.ds(3, tile_rows), tile_cols:, :] = slab.reshape(tile_rows, tile_cols, width)
    for first, at in ((0, tile_rows + 3), (2, 0)):
        slab = dot(corner, cornrecv[first : first + 2].reshape(32, width)).astype(BF16)
        pad[at : at + 3, tile_cols:, :] = slab.reshape(3, tile_cols, width)

    for group in range(pad.shape[0] // 8):
        moved = dot(shift_sel[...], pad[8 * group : 8 * group + 8].reshape(8 * wide, width))
        shifted[:, 8 * group : 8 * group + 8] = moved.reshape(7, 8, tile_cols, width)

    scale = gain[...]
    half = width // 2

    for g in range(tile_cols // 8):
        for lanes in (slice(0, half), slice(half, width)):

            def rows_step(step, carry):
                r0 = step * 16
                acc = [jnp.zeros((8, half), F32) for _ in range(16)]
                for dc in range(7):
                    taps = [
                        jnp.broadcast_to(dwf[dr, dc : dc + 1, lanes], (8, half))
                        for dr in range(7)
                    ]
                    for i in range(22):
                        x = shifted[dc, r0 + i, 8 * g : 8 * g + 8, lanes]
                        for dr in range(7):
                            o = i - dr
                            if 0 <= o < 16:
                                acc[o] = acc[o] + x * taps[dr]
                for o in range(16):
                    conv[r0 + o, 8 * g : 8 * g + 8, lanes] = acc[o]
                return carry

            lax.fori_loop(0, tile_rows // 16, rows_step, 0, unroll=True)

    normed = layer_norm(conv[...].reshape(pixels, width))
    image = feat[...].astype(F32).reshape(pixels, width)
    result = (image + normed * scale).astype(BF16)
    mem[...] = result.reshape(tile_rows, tile_cols, width)

    loads["wk"].wait()
    loads["wv"].wait()
    flat = mem[...].reshape(pixels, width)
    keys[...] = dot(flat, wk[...]).astype(BF16)
    values[...] = dot(flat, wv[...]).astype(BF16)

    def attend(index):
        q = queries[pl.ds(pl.multiple_of(index * block, 16), block), :]
        head_of = iota((block, width), 1) // head_dim
        spread = jnp.concatenate(
            [jnp.where(head_of == h, q, jnp.zeros_like(q)) for h in range(HEADS)], axis=0
        )
        scores = lax.dot_general(
            spread, keys[...], (((1,), (1,)), ((), ())), preferred_element_type=F32
        )
        top = jnp.max(scores, axis=-1, keepdims=True)
        expo = jnp.exp(scores - top)
        total = jnp.sum(expo, axis=-1, keepdims=True)
        out = dot(expo.astype(BF16), values[...])
        sums = jnp.zeros((block, width), F32)
        maxima = jnp.zeros((block, width), F32)
        totals = jnp.zeros((block, width), F32)
        for h in range(HEADS):
            rows = slice(h * block, (h + 1) * block)
            here = head_of == h
            sums = jnp.where(here, out[rows], sums)
            maxima = jnp.where(here, top[rows], maxima)
            totals = jnp.where(here, total[rows], totals)
        return sums, maxima, totals

    def p1(k):
        return pltpu.make_async_remote_copy(
            src_ref=p1send.at[k - 1], dst_ref=p1recv.at[k - 1],
            send_sem=s1.at[k - 1], recv_sem=r1.at[k - 1],
            device_id={SCATTER: lax.rem(me_a + k, n_a)}, device_id_type=MESH,
        )

    def scatter_step(step, carry):
        k = step + 1
        pack(to_stats, p1send.at[step], *attend(lax.rem(me_a + k, n_a)))
        p1(k).start()
        return carry

    lax.fori_loop(0, n_a - 1, scatter_step, 0)
    parts = [attend(me_a)]
    for k in range(1, n_a):
        p1(k).wait_recv()
        parts.append(unpack(to_wide, p1recv.at[k - 1], block))
    mine = combine(parts)
    pack(to_stats, p2send, *mine)

    def p2(k):
        return pltpu.make_async_remote_copy(
            src_ref=p2send, dst_ref=p2recv.at[k - 1],
            send_sem=s2.at[k - 1], recv_sem=r2.at[k - 1],
            device_id={EXCHANGE: lax.rem(me_b + k, n_b)}, device_id_type=MESH,
        )

    for k in range(1, n_b):
        p2(k).start()
    parts = [unpack(to_wide, p2send, block)]
    for k in range(1, n_b):
        p2(k).wait_recv()
        parts.append(unpack(to_wide, p2recv.at[k - 1], block))
    sums, _, totals = combine(parts)
    attended[me_a] = (sums / totals).astype(BF16)

    def p3(k):
        return pltpu.make_async_remote_copy(
            src_ref=attended.at[me_a], dst_ref=attended.at[me_a],
            send_sem=s3.at[k - 1], recv_sem=r3.at[k - 1],
            device_id={SCATTER: lax.rem(me_a + k, n_a)}, device_id_type=MESH,
        )

    for k in range(1, n_a):
        p3(k).start()
    for k in range(1, n_a):
        p3(k).wait_recv()
    loads["wo"].wait()
    projected = dot(attended[...].reshape(n_a * block, width), wo[...])
    dec[...] = layer_norm(qs[...].astype(F32) + projected[:n_query])

    for index in range(8):
        copy, there, comes, dst = halos[index]

        @pl.when(there)
        def _():
            copy.wait_send()

    for k in range(1, n_a):
        p1(k).wait_send()
        p3(k).wait_send()
    for k in range(1, n_b):
        p2(k).wait_send()


def body(sizes, features, dw_kernel, norm_gain, query_state, query_pos, wq, wk, wv, wo):
    tile_rows, tile_cols, width = features.shape
    n_query = query_state.shape[0]
    n_a, n_b = sizes[SCATTER], sizes[EXCHANGE]
    block = -(-n_query // (16 * n_a)) * 16
    pixels = tile_rows * tile_cols
    message = block + stat_rows(block)
    vmem = pl.BlockSpec(memory_space=pltpu.VMEM)
    dma = pltpu.SemaphoreType.DMA
    given = (
        features, dw_kernel, norm_gain.reshape(1, width), query_state, query_pos, wq, wk, wv, wo
    )
    return pl.pallas_call(
        functools.partial(kernel, sizes),
        out_shape=(
            jax.ShapeDtypeStruct(features.shape, BF16),
            jax.ShapeDtypeStruct((n_query, width), F32),
        ),
        in_specs=[pl.BlockSpec(memory_space=pltpu.HBM)] * 9,
        out_specs=(vmem, vmem),
        scratch_shapes=[pltpu.VMEM(x.shape, x.dtype) for x in given] + [
            dma((9,)),
            pltpu.VMEM((TERMS, width, width), BF16),
            pltpu.VMEM((2, width, width), BF16),
            pltpu.VMEM((tile_rows + 8, 2 * tile_cols, width), BF16),
            pltpu.VMEM((7, tile_rows + 8, tile_cols, width), F32),
            pltpu.VMEM((7 * 8 * tile_cols, 16 * tile_cols), BF16),
            pltpu.VMEM((pixels, 6 * tile_rows), BF16),
            pltpu.VMEM((7, 7, width), F32),
            pltpu.VMEM((tile_rows, tile_cols, width), F32),
            pltpu.VMEM((6 * tile_rows + 64, width), BF16),
            pltpu.VMEM((2, 3, tile_cols, width), BF16),
            pltpu.VMEM((2, 3 * tile_rows, width), BF16),
            pltpu.VMEM((4, 16, width), BF16),
            pltpu.VMEM((pixels, width), BF16),
            pltpu.VMEM((pixels, width), BF16),
            pltpu.VMEM((n_a * block, width), F32),
            pltpu.VMEM((n_a * block, width), BF16),
            pltpu.VMEM((n_a - 1, message, width), BF16),
            pltpu.VMEM((n_a - 1, message, width), BF16),
            pltpu.VMEM((message, width), BF16),
            pltpu.VMEM((n_b - 1, message, width), BF16),
            pltpu.VMEM((n_a, block, width), BF16),
            dma((8,)), dma((8,)),
            dma((n_a - 1,)), dma((n_a - 1,)),
            dma((n_b - 1,)), dma((n_b - 1,)),
            dma((n_a - 1,)), dma((n_a - 1,)),
        ],
        compiler_params=pltpu.CompilerParams(
            collective_id=0, has_side_effects=True, vmem_limit_bytes=62 * 1024 * 1024
        ),
    )(*given)


def solution(mesh):
    sizes = dict(mesh.shape)
    in_specs = (
        P(("scenes", "rows"), "cols", None),
        P(),
        P(),
        P("scenes", None),
        P("scenes", None),
        P(),
        P(),
        P(),
        P(),
    )
    out_specs = (P(("scenes", "rows"), "cols", None), P("scenes", None))
    return jax.shard_map(
        functools.partial(body, sizes), mesh=mesh, in_specs=in_specs, out_specs=out_specs,
        check_vma=False,
    )
```
